32 devices in a mesh: groups: 2 (over y), rows: 4 (over z), reps: 2 (over x), cols: 2 (over core).
Axes of the slice: x: 2, y: 2, z: 4, core: 2. Of those that a mesh axis runs over, the one named last changes fastest.
Arguments:
- scalars: bfloat16 [256, 4096], P(None, ('groups', 'rows', 'reps', 'cols')), parts along dimension 1, may hold values from -6 to 6
- vectors: bfloat16 [3, 64, 4096], P(None, None, ('groups', 'rows', 'reps', 'cols')), parts along dimension 2, may hold values from -6 to 6
- positions: bfloat16 [3, 4096], P(None, ('groups', 'rows', 'reps', 'cols')), parts along dimension 1, may hold values from -5 to 5
- node_pose: int32 [4096], P(('groups', 'rows', 'reps', 'cols')), parts along dimension 0, may hold values from 0 to 3, never falling along the last dimension, each value on 1 to 768 neighbouring positions
- source_block: int32 [512], P(('groups', 'rows', 'reps', 'cols')), parts along dimension 0, may hold values from 0 to 15, as said below
- target_block: int32 [512], P(('groups', 'rows', 'reps', 'cols')), parts along dimension 0, may hold values from 0 to 15, as said below
- block_count: int32 [32], P(('groups', 'rows', 'reps', 'cols')), parts along dimension 0, may hold values from 11 to 16, as said below
- shell_codes: int32 [512, 128, 128], P(('groups', 'rows', 'reps', 'cols')), parts along dimension 0, may hold values from 0 to 10
- weight_in: bfloat16 [256, 256], replicated, may hold values from -0.375 to 0.375
- message_weight: bfloat16 [384, 256], replicated, may hold values from -0.375 to 0.375
- filter_weights: bfloat16 [10, 384], replicated, may hold values from -0.125 to 0.125
- read_scalar: float32 [256], replicated, may hold values from -4 to 4
- read_vector: float32 [64], replicated, may hold values from -0.12 to 0.12
- targets: float32 [8], P('groups'), parts along dimension 0, may hold values from -6 to 6
Outputs:
- new_scalars: bfloat16 [256, 4096], P(None, ('groups', 'rows', 'reps', 'cols')), parts along dimension 1
- new_vectors: bfloat16 [3, 64, 4096], P(None, None, ('groups', 'rows', 'reps', 'cols')), parts along dimension 2
- scores: float32 [8], P('groups'), parts along dimension 0
- forces: float32 [3, 4096], P(None, ('groups', 'rows', 'reps', 'cols')), parts along dimension 1
The draws below stay inside these ranges and needn't reach their ends.
There are 2 independent parts, one for each index of `groups`. The reference program is written for one: setup_inputs(seed, part) draws one part's arguments, and reference() takes and returns one part's arrays. A program takes and returns all parts, laid end to end along the dimension named above; an argument that names none is the same for every part. Nothing has to cross between parts.
Inputs may be any that keep to these rules, and one draw needn't show every extreme that they name: With g = e // 16: source_block[e] // 4 equals g // 4, and source_block[e] % 2 equals g % 2. With g = e // 16: (target_block[e] // 2) % 2 equals (g // 2) % 2. Two slots of one group whose offsets within the group differ by less than 8 name different target blocks. block_count[g] counts the live slots g * 16 to g * 16 + block_count[g] - 1; some group has all 16 live. node_pose never falls along the atoms; every pose has 1 to 768 atoms, one exactly 768.
All inputs are finite; a program needn't handle non-finite values.
Results may differ from the reference program's by a relative error of at most 0.017.
Values may be sent and summed in bfloat16 or wider, within the bound.
A program may use at most 128 MiB of HBM per device.

```python
import math
import jax
import jax.numpy as jnp
import numpy as np
from jax import lax

S_CH = 256
V_CH = 64
SHELLS = 10
BLK = 128
EB = 16
POSE_ATOMS = 512
DEVS = 16
NODES = 2048
SLOTS = 256
POSES = 4
POSE_MOST = 768
N_ROWS = 4
N_REPS = 2
N_COLS = 2


def draw_source_block(key, part):
    key = jax.random.fold_in(key, 11)
    group = jnp.arange(EB * DEVS, dtype=jnp.int32) // EB
    row_index = group // (N_REPS * N_COLS)
    col_index = group % N_COLS
    chosen = jax.random.randint(key, (EB * DEVS,), 0, N_REPS, dtype=jnp.int32)
    return (row_index * N_REPS + chosen) * N_COLS + col_index


def draw_target_block(key, part):
    key = jax.random.fold_in(key, 23)
    place_count = N_ROWS * N_COLS
    scores = jax.random.randint(key, (DEVS, place_count), 0, 1048576, dtype=jnp.int32) * place_count + jnp.arange(place_count, dtype=jnp.int32)[None, :]
    orders = jnp.argsort(scores, axis=1, stable=True).astype(jnp.int32)
    slot_index = jnp.arange(EB * DEVS, dtype=jnp.int32)
    group = slot_index // EB
    offset = slot_index % EB
    place = orders[group, offset % place_count]
    row_pick = place // N_COLS
    col_pick = place % N_COLS
    rep_index = group // N_COLS % N_REPS
    return (row_pick * N_REPS + rep_index) * N_COLS + col_pick


def draw_block_count(key, part):
    key = jax.random.fold_in(key, 37)
    first_key, second_key = jax.random.split(key)
    lowest = EB - max(1, 5 * EB // 16)
    counts = jax.random.randint(first_key, (DEVS,), lowest, EB + 1, dtype=jnp.int32)
    busiest = jax.random.randint(second_key, (), 0, DEVS, dtype=jnp.int32)
    return jnp.where(jnp.arange(DEVS, dtype=jnp.int32) == busiest, EB, counts)


def touch_ends(result, stream_key, smallest, top_value):
    dims = result.shape
    spot = [jax.random.randint(jax.random.fold_in(stream_key, axis), (), 0, dims[axis]) for axis in range(len(dims))]
    result = result.at[tuple(spot)].set(smallest)
    longest = dims.index(max(dims))
    spot[longest] = (spot[longest] + 1) % dims[longest]
    return result.at[tuple(spot)].set(top_value)


def block_levels(key, shape, cuts, smallest, largest):
    gain, own = 1.0, jax.random.fold_in(key, 6)
    for dim, shards_of in cuts:
        draws = jnp.exp(jax.random.uniform(jax.random.fold_in(own, dim), (shards_of,), jnp.float32, smallest / len(cuts), largest / len(cuts)))
        gain = gain * jnp.repeat(draws, shape[dim] // shards_of).reshape([-1 if axis == dim else 1 for axis in range(len(shape))])
    return gain


def length_profile(amount, total, bound, lean):
    portions = [(1 << 20) // math.isqrt(grade ** lean) + 1 for grade in range(2, amount + 1)]
    spare, given = total - bound - (amount - 1), [1] * (amount - 1)
    while spare > 0:
        free = [i for i in range(amount - 1) if given[i] < bound]
        pool, left = sum([portions[i] for i in free]), spare
        for i in free:
            addition = min(bound - given[i], max(1, left * portions[i] // pool), spare)
            given[i] = given[i] + addition
            spare = spare - addition
    return np.array([bound] + given)


def uneven(rng, number_of, total, most, lean):
    if number_of == 2:
        one = jax.random.randint(rng, (), max(1, total - most), min(most, total - 1) + 1)
        return jnp.stack([one, total - one])
    sizes = jnp.asarray(length_profile(number_of, total, most, lean), jnp.int32)
    couples = (number_of - 1) // 2
    donor, sink = sizes[1:1 + 2 * couples:2], sizes[2:2 + 2 * couples:2]
    margin = jnp.minimum(donor - 1, most - sink)
    shifted = jax.random.randint(jax.random.fold_in(rng, 1), (couples,), 0, 1 << 20) % (margin + 1)
    sizes = sizes.at[1:1 + 2 * couples:2].set(donor - shifted).at[2:2 + 2 * couples:2].set(sink + shifted)
    return sizes[jax.random.permutation(jax.random.fold_in(rng, 2), number_of)]


def scatter_about(rng, shape, width, bound, cuts=(), held_as=jnp.bfloat16):
    result = width * jax.random.normal(rng, shape, jnp.float32)
    if cuts:
        result = result * block_levels(rng, shape, cuts, -0.22, 0.18)
    return jnp.clip(result, -bound, bound).astype(held_as)


def setup_inputs(seed: int = 0, part: int = 0) -> dict:
    keys = jax.random.split(jax.random.key(seed), 15)
    part_splits = jax.random.split(jax.random.fold_in(keys[14], part), 15)
    return {
        "scalars": scatter_about(part_splits[0], (S_CH, NODES), 1.0, 6.0, ((1, 16),)),
        "vectors": scatter_about(part_splits[1], (3, V_CH, NODES), 1.0, 6.0, ((2, 16),)),
        "positions": scatter_about(part_splits[2], (3, NODES), 1.0, 5.0, ((1, 16),)),
        "node_pose": jnp.searchsorted(jnp.cumsum(uneven(part_splits[3], POSES, NODES, POSE_MOST, 1)), jnp.arange(NODES), side="right").astype(jnp.int32),
        "source_block": draw_source_block(jax.random.fold_in(jax.random.fold_in(keys[14], part), 71), part),
        "target_block": draw_target_block(jax.random.fold_in(jax.random.fold_in(keys[14], part), 71), part),
        "block_count": draw_block_count(jax.random.fold_in(jax.random.fold_in(keys[14], part), 71), part),
        "shell_codes": touch_ends(jax.random.randint(part_splits[7], (SLOTS, BLK, BLK), 0, SHELLS + 1), jax.random.fold_in(part_splits[7], 1), 0, SHELLS).astype(jnp.int32),
        "weight_in": scatter_about(keys[8], (S_CH, S_CH), S_CH ** -0.5, 0.375),
        "message_weight": scatter_about(keys[9], (S_CH + 2 * V_CH, S_CH), S_CH ** -0.5, 0.375),
        "filter_weights": scatter_about(keys[10], (SHELLS, S_CH + 2 * V_CH), (EB * BLK) ** -0.5, 0.125),
        "read_scalar": scatter_about(keys[11], (S_CH,), 1.0, 4.0, (), jnp.float32),
        "read_vector": scatter_about(keys[12], (V_CH,), 0.03, 0.12, (), jnp.float32),
        "targets": scatter_about(part_splits[13], (POSES,), 1.5, 6.0, (), jnp.float32),
    }


def filtered(gates, vectors, positions, filter_weights, scalar_width, vector_width):
    weights_t = filter_weights.astype(jnp.float32).T
    gates = gates.astype(jnp.float32)
    vectors = vectors.astype(jnp.float32)
    positions = positions.astype(jnp.float32)
    scalar_part = gates[..., :scalar_width, None, :] * weights_t[:scalar_width, :, None]
    gate_vec = gates[..., scalar_width:scalar_width + vector_width, :]
    gate_pos = gates[..., scalar_width + vector_width:, :]
    vector_part = (gate_vec[..., None, :, None, :] * vectors[..., :, :, None, :]) * weights_t[scalar_width:scalar_width + vector_width, :, None]
    vector_part = vector_part + (gate_pos[..., None, :, None, :] * positions[..., :, None, None, :]) * weights_t[scalar_width + vector_width:, :, None]
    norm_part = gate_pos[..., :, None, :] * weights_t[scalar_width + vector_width:, :, None]
    leading = gates.shape[:-2]
    columns = weights_t.shape[1] * gates.shape[-1]
    stacked = jnp.concatenate([scalar_part.reshape(leading + (scalar_width, columns)), vector_part.reshape(leading + (3 * vector_width, columns)), norm_part.reshape(leading + (vector_width, columns))], axis=-2)
    return stacked.astype(jnp.bfloat16)


def one_hot_shells(shell_block, shell_count):
    levels = jnp.arange(1, shell_count + 1, dtype=jnp.int32)
    return (shell_block[None, :, :] == levels[:, None, None]).astype(jnp.bfloat16)


def message_inputs(scalars, weight_in, message_weight):
    hidden = jax.nn.silu(jnp.einsum("oi,...ib->...ob", weight_in, scalars, preferred_element_type=jnp.float32)).astype(jnp.bfloat16)
    return jnp.einsum("oi,...ib->...ob", message_weight, hidden, preferred_element_type=jnp.float32).astype(jnp.bfloat16)


def reference(scalars, vectors, positions, node_pose, source_block, target_block, block_count, shell_codes, weight_in, message_weight, filter_weights, read_scalar, read_vector, targets):
    block_total = NODES // BLK
    out_rows = S_CH + 4 * V_CH
    group_total = N_ROWS * N_REPS * N_COLS
    gates = message_inputs(scalars, weight_in, message_weight)
    gate_blocks = gates.reshape(S_CH + 2 * V_CH, block_total, BLK).transpose(1, 0, 2)
    vector_blocks = vectors.reshape(3, V_CH, block_total, BLK).transpose(2, 0, 1, 3)
    position_blocks = positions.reshape(3, block_total, BLK).transpose(1, 0, 2)

    def group_step(message_blocks, group):
        rep_index = (group // N_COLS) % N_REPS

        def slot_step(totals, offset):
            slot = group * EB + offset
            source = source_block[slot]
            target = target_block[slot]
            live = (offset < block_count[group]).astype(jnp.bfloat16)
            table = one_hot_shells(shell_codes[slot], SHELLS).reshape(SHELLS * BLK, BLK) * live
            left = filtered(gate_blocks[source], vector_blocks[source], position_blocks[source], filter_weights, S_CH, V_CH)
            term = jnp.dot(left, table, preferred_element_type=jnp.float32)
            place = (target // (N_REPS * N_COLS)) * N_COLS + target % N_COLS
            return totals.at[place].add(term), None

        totals, _ = lax.scan(slot_step, jnp.zeros((N_ROWS * N_COLS, out_rows, BLK), jnp.float32), jnp.arange(EB, dtype=jnp.int32))
        rounded = lax.optimization_barrier(totals.astype(jnp.bfloat16)).astype(jnp.float32)
        places = ((jnp.arange(N_ROWS, dtype=jnp.int32)[:, None] * N_REPS + rep_index) * N_COLS + jnp.arange(N_COLS, dtype=jnp.int32)[None, :]).reshape(-1)
        return message_blocks.at[places].add(rounded), None

    message_blocks, _ = lax.scan(group_step, jnp.zeros((block_total, out_rows, BLK), jnp.float32), jnp.arange(group_total, dtype=jnp.int32))
    message = message_blocks.transpose(1, 0, 2).reshape(out_rows, NODES)
    delta_vec = message[S_CH:S_CH + 3 * V_CH].reshape(3, V_CH, NODES)
    norm_term = message[S_CH + 3 * V_CH:]
    new_scalars = (scalars.astype(jnp.float32) + message[:S_CH]).astype(jnp.bfloat16)
    new_vectors = (vectors.astype(jnp.float32) + delta_vec - positions.astype(jnp.float32)[:, None, :] * norm_term[None]).astype(jnp.bfloat16)
    scalar_float = new_scalars.astype(jnp.float32)
    vector_float = new_vectors.astype(jnp.float32)
    energy = jnp.sum(read_scalar[:, None] * scalar_float, axis=0) + jnp.sum(read_vector[:, None] * jnp.sum(vector_float * vector_float, axis=0), axis=0)
    scores = jax.ops.segment_sum(energy, node_pose, num_segments=POSES) / POSE_ATOMS
    node_resid = (scores - targets)[node_pose]
    grad_vec = (2.0 * node_resid[None, None, :] * read_vector[None, :, None] * vector_float).astype(jnp.bfloat16)
    grad_blocks = grad_vec.reshape(3 * V_CH, block_total, BLK).transpose(1, 0, 2)
    weight_rows = jnp.tile(filter_weights[:, S_CH + V_CH:].astype(jnp.float32), (1, 3)).T

    def back_step(totals, slot):
        group = slot // EB
        live = ((slot % EB) < block_count[group]).astype(jnp.float32)
        table = one_hot_shells(shell_codes[slot], SHELLS).astype(jnp.float32) * live
        product = jnp.einsum("ri,kji->rkj", grad_blocks[target_block[slot]].astype(jnp.float32), table, precision=lax.Precision.HIGHEST)
        term = jnp.sum(product * weight_rows[:, :, None], axis=1)
        return totals.at[source_block[slot]].add(term), None

    back_blocks, _ = lax.scan(back_step, jnp.zeros((block_total, 3 * V_CH, BLK), jnp.float32), jnp.arange(EB * group_total, dtype=jnp.int32))
    back = back_blocks.transpose(1, 0, 2).reshape(3, V_CH, NODES)
    gate_pos = gates[S_CH + V_CH:].astype(jnp.float32)
    forces = jnp.sum(norm_term[None] * grad_vec.astype(jnp.float32), axis=1) - jnp.sum(gate_pos[None] * back, axis=1)
    return new_scalars, new_vectors, scores, forces
```

```python
import functools

import jax
import jax.numpy as jnp
from jax import lax
from jax.experimental import pallas as pl
from jax.experimental.pallas import tpu as pltpu
from jax.sharding import PartitionSpec as P

POSE_ATOMS = 512
BF = jnp.bfloat16
F32 = jnp.float32
MESH = pl.DeviceIdType.MESH
HIGHEST = lax.Precision.HIGHEST


def kernel(
    rows, reps, cols, poses, shells,
    scalars, vectors, positions, node_pose, source_block, target_block, block_count, codes_hbm,
    weight_in, message_weight, filter_weights, read_scalar, read_vector, targets,
    out_scalars, out_vectors, out_scores, out_forces,
    codes, panel_s, panel_v, panel_p, gate_pos, rows_f, fwb, rv_col, xsend, xrecv, own, ssend, recv,
    norm_buf, gather, energies, force_acc, force_recv, force_norm,
    codes_sem, panel_send, panel_recv, x_send, x_recv, s_send, s_recv,
    g_send, g_recv, f_send, e_send, e_recv, q_send, q_recv,
):
    row = lax.axis_index("rows")
    rep = lax.axis_index("reps")
    col = lax.axis_index("cols")
    total = rows * reps * cols
    me = (row * reps + rep) * cols + col
    s_ch = scalars.shape[0]
    v3 = vectors.shape[0]
    v_ch = v3 // 3
    blk = scalars.shape[1]
    slots = codes.shape[0]
    places = rows * cols
    windows = -(-slots // places)
    pose_pad = energies.shape[1]

    def peer(q):
        flat = lax.rem(me + q, total)
        return flat, {
            "rows": flat // (reps * cols),
            "reps": lax.rem(flat // cols, reps),
            "cols": lax.rem(flat, cols),
        }

    barrier = pltpu.get_barrier_semaphore()

    def greet(q, carry):
        pl.semaphore_signal(barrier, inc=1, device_id=peer(q)[1], device_id_type=MESH)
        return carry

    lax.fori_loop(1, total, greet, 0)
    codes_copy = pltpu.make_async_copy(codes_hbm, codes, codes_sem)
    codes_copy.start()

    panel_p[rep] = jnp.zeros((8, blk), F32)
    panel_p[rep, 0:3, :] = positions[...].astype(F32)
    panel_s[rep] = scalars[...]
    panel_v[rep] = vectors[...]
    lane_shell = lax.broadcasted_iota(jnp.int32, (shells, shells * blk), 1) // blk
    sub_shell = lax.broadcasted_iota(jnp.int32, (shells, shells * blk), 0)
    spread = jnp.where(lane_shell == sub_shell, 1.0, 0.0).astype(BF)
    fwb[...] = lax.dot_general(
        filter_weights[...], spread, (((0,), (0,)), ((), ())), preferred_element_type=F32
    )
    rv_row = jnp.concatenate([read_vector[...], jnp.zeros((1, 128 - v_ch), F32)], axis=1)
    rv_col[...] = jnp.transpose(jnp.broadcast_to(rv_row, (blk, 128)))[:v_ch]

    pl.semaphore_wait(barrier, total - 1)

    def panel_copies(q, src_rep):
        out = []
        for a, buf in enumerate((panel_s, panel_v, panel_p)):
            out.append(
                pltpu.make_async_remote_copy(
                    src_ref=buf.at[src_rep],
                    dst_ref=buf.at[src_rep],
                    send_sem=panel_send.at[a, q],
                    recv_sem=panel_recv.at[a, src_rep],
                    device_id={"reps": q},
                    device_id_type=MESH,
                )
            )
        return out

    for o in range(1, reps):
        for c in panel_copies(lax.rem(rep + o, reps), rep):
            c.start()

    def make_rows(q):
        hidden = jnp.dot(weight_in[...], panel_s[q], preferred_element_type=F32)
        hidden = (hidden / (1.0 + jnp.exp(-hidden))).astype(BF)
        gates = jnp.dot(message_weight[...], hidden, preferred_element_type=F32).astype(BF)
        gates = gates.astype(F32)
        gs = gates[:s_ch]
        gv = gates[s_ch : s_ch + v_ch]
        gp = gates[s_ch + v_ch :]
        gate_pos[q] = gp
        pos = panel_p[q]
        vec = panel_v[q].astype(F32)
        gvv = [gv * vec[d * v_ch : (d + 1) * v_ch] for d in range(3)]
        gpp = [gp * pos[d : d + 1] for d in range(3)]
        for k in range(shells):
            span = pl.ds(k * blk, blk)
            rows_f[q, 0:s_ch, span] = (gs * fwb[0:s_ch, span]).astype(BF)
            wv = fwb[s_ch : s_ch + v_ch, span]
            wp = fwb[s_ch + v_ch :, span]
            for d in range(3):
                rows_f[q, s_ch + d * v_ch : s_ch + (d + 1) * v_ch, span] = (
                    gvv[d] * wv + gpp[d] * wp
                ).astype(BF)
            rows_f[q, s_ch + v3 :, span] = (gp * wp).astype(BF)

    def rows_step(o, carry):
        q = lax.rem(rep + o, reps)

        @pl.when(o > 0)
        def _():
            for c in panel_copies(q, q):
                c.wait_recv()

        make_rows(q)
        return carry

    lax.fori_loop(0, reps, rows_step, 0)
    codes_copy.wait()

    def find(r, c, t):
        wanted = (r * reps + rep) * cols + c
        slot = jnp.int32(0)
        found = jnp.int32(0)
        for o in range(t * places, min((t + 1) * places, slots)):
            hit = (target_block[o] == wanted) & (o < block_count[0])
            slot = jnp.where(hit, o, slot)
            found = jnp.where(hit, 1, found)
        src = lax.rem(source_block[slot] // cols, reps)
        return codes[slot] * found, src

    def one_hot(code, axis):
        return jnp.concatenate(
            [jnp.where(code == k + 1, 1.0, 0.0).astype(BF) for k in range(shells)], axis=axis
        )

    def partial(r, c):
        acc = None
        for t in range(windows):
            code, src = find(r, c, t)
            term = jnp.dot(rows_f[src], one_hot(code, 0), preferred_element_type=F32)
            acc = term if acc is None else acc + term
        return acc

    def row_of(s):
        offset = 1 + lax.rem(rows // 2 - 1 + s, rows - 1)
        return lax.rem(row + jnp.where(s == rows - 1, 0, offset), rows)

    def cross(s, o, arriving):
        if arriving:
            mine = o - 1
        else:
            mine = cols - o - 1
        return pltpu.make_async_remote_copy(
            src_ref=xsend.at[s, o - 1],
            dst_ref=xrecv.at[s, mine],
            send_sem=x_send.at[s, o - 1],
            recv_sem=x_recv.at[s, mine],
            device_id={"cols": lax.rem(col + o, cols)},
            device_id_type=MESH,
        )

    def along(s, src_row):
        return pltpu.make_async_remote_copy(
            src_ref=ssend.at[s],
            dst_ref=recv.at[src_row],
            send_sem=s_send.at[s],
            recv_sem=s_recv.at[src_row],
            device_id={"rows": row_of(s)},
            device_id_type=MESH,
        )

    def finish(s):
        for o in range(1, cols):
            cross(s, o, True).wait_recv()
        both = own[s]
        for o in range(1, cols):
            both = both + xrecv[s, o - 1].astype(F32)
        return both

    def forward_step(s, carry):
        r = row_of(s)
        for o in range(1, cols):
            xsend[s, o - 1] = partial(r, lax.rem(col + o, cols)).astype(BF)
            cross(s, o, False).start()

        @pl.when(s > 0)
        def _():
            ssend[s - 1] = finish(s - 1).astype(BF)
            along(s - 1, row).start()

        own[s] = partial(r, col)
        return carry

    lax.fori_loop(0, rows, forward_step, 0)
    last = rows - 1
    own[last] = finish(last)
    for s in range(rows - 1):
        along(s, row_of(s)).wait_recv()

    def message(lo, hi):
        acc = own[last, lo:hi]
        for s in range(rows - 1):
            acc = acc + recv[row_of(s), lo:hi].astype(F32)
        return acc

    norm = message(s_ch + v3, s_ch + v3 + v_ch)
    norm_buf[...] = norm
    pos_own = panel_p[rep]
    square = jnp.zeros((v_ch, blk), F32)
    for d in range(3):
        lo = d * v_ch
        nv = (
            vectors[lo : lo + v_ch].astype(F32)
            + message(s_ch + lo, s_ch + lo + v_ch)
            - pos_own[d : d + 1] * norm
        ).astype(BF)
        out_vectors[lo : lo + v_ch] = nv
        gather[row, col, lo : lo + v_ch] = nv
        nv = nv.astype(F32)
        square = square + nv * nv
    pose_row = node_pose[...]
    gather[row, col, v3 : v3 + 16] = jnp.broadcast_to(pose_row.astype(F32), (16, blk)).astype(BF)

    def spread_row(o, src_row):
        return pltpu.make_async_remote_copy(
            src_ref=gather.at[src_row, col],
            dst_ref=gather.at[src_row, col],
            send_sem=g_send.at[o],
            recv_sem=g_recv.at[src_row, col],
            device_id={"rows": lax.rem(row + o, rows)},
            device_id_type=MESH,
        )

    def spread_col(s, o, src_row, src_col):
        return pltpu.make_async_remote_copy(
            src_ref=gather.at[src_row, src_col],
            dst_ref=gather.at[src_row, src_col],
            send_sem=f_send.at[s, o - 1],
            recv_sem=g_recv.at[src_row, src_col],
            device_id={"cols": lax.rem(col + o, cols)},
            device_id_type=MESH,
        )

    for i in range(rows - 1):
        o = 1 + (rows // 2 - 1 + i) % (rows - 1)
        spread_row(o, row).start()
    for o in range(1, cols):
        spread_col(0, o, row, col).start()

    ns = (scalars[...].astype(F32) + message(0, s_ch)).astype(BF)
    out_scalars[...] = ns
    energy = jnp.dot(
        read_scalar[...], ns.astype(F32), preferred_element_type=F32, precision=HIGHEST
    ) + jnp.dot(read_vector[...], square, preferred_element_type=F32, precision=HIGHEST)
    pose_iota = lax.broadcasted_iota(jnp.int32, (pose_pad, blk), 0)
    energies[me] = jnp.where(
        jnp.broadcast_to(pose_row, (pose_pad, blk)) == pose_iota,
        jnp.broadcast_to(energy, (pose_pad, blk)),
        0.0,
    )

    def energy_copy(q, src):
        return pltpu.make_async_remote_copy(
            src_ref=energies.at[src],
            dst_ref=energies.at[src],
            send_sem=e_send.at[q],
            recv_sem=e_recv.at[src],
            device_id=peer(q)[1],
            device_id_type=MESH,
        )

    def energy_start(q, carry):
        energy_copy(q, me).start()
        return carry

    def energy_wait(q, carry):
        energy_copy(q, peer(q)[0]).wait_recv()
        return carry

    lax.fori_loop(1, total, energy_start, 0)
    force_acc[...] = jnp.zeros_like(force_acc)
    lax.fori_loop(1, total, energy_wait, 0)
    sums = energies[0]
    for q in range(1, total):
        sums = sums + energies[q]
    scores = jnp.broadcast_to(
        jnp.sum(sums, axis=1, keepdims=True) / POSE_ATOMS, (pose_pad, blk)
    )
    lane_iota = lax.broadcasted_iota(jnp.int32, (pose_pad, blk), 1)
    score_row = jnp.sum(jnp.where(lane_iota == pose_iota, scores, 0.0), axis=0, keepdims=True)
    out_scores[...] = score_row[:, :poses]
    wanted = jnp.zeros((pose_pad, blk), F32)
    for p in range(poses):
        wanted = jnp.where(pose_iota == p, targets[p], wanted)
    resid = scores - wanted

    def gradient(r, c):
        pose = gather[r, c, v3 : v3 + 16].astype(F32)[0:1]
        member = jnp.broadcast_to(pose, (pose_pad, blk)) == pose_iota.astype(F32)
        node_resid = jnp.sum(jnp.where(member, resid, 0.0), axis=0, keepdims=True)
        scale = 2.0 * node_resid * rv_col[...]
        return [
            (scale * gather[r, c, d * v_ch : (d + 1) * v_ch].astype(F32)).astype(BF).astype(F32)
            for d in range(3)
        ]

    own_grad = gradient(row, col)
    for d in range(3):
        force_norm[d : d + 1] = jnp.sum(norm_buf[...] * own_grad[d], axis=0, keepdims=True)

    def backward(r, c):
        grad = gradient(r, c)
        weights = [fwb[s_ch + v_ch :, k * blk : (k + 1) * blk] for k in range(shells)]
        left = jnp.concatenate(
            [
                jnp.concatenate([(grad[d] * w).astype(BF) for w in weights], axis=1)
                for d in range(3)
            ],
            axis=0,
        )
        found = [find(r, c, t) for t in range(windows)]
        table = jnp.concatenate([one_hot(code, 1) for code, _ in found], axis=0)
        back = lax.dot_general(
            left, table, (((1,), (1,)), ((), ())), preferred_element_type=F32
        )
        for t, (_, src) in enumerate(found):
            gp = gate_pos[src]
            for d in range(3):
                piece = back[d * v_ch : (d + 1) * v_ch, t * blk : (t + 1) * blk]
                term = jnp.sum(gp * piece, axis=0, keepdims=True)
                for q in range(reps):
                    force_acc[q, d : d + 1] += jnp.where(src == q, term, 0.0)

    def backward_step(s, carry):
        r = lax.rem(row + s, rows)

        @pl.when(s > 0)
        def _():
            spread_row(1, r).wait_recv()
            for o in range(1, cols):
                spread_col(s, o, r, col).start()

        backward(r, col)
        for o in range(1, cols):
            c = lax.rem(col + o, cols)
            spread_col(s, o, r, c).wait_recv()
            backward(r, c)
        return carry

    lax.fori_loop(0, rows, backward_step, 0)

    def force_copy(o, src):
        return pltpu.make_async_remote_copy(
            src_ref=force_acc.at[lax.rem(rep + o, reps)],
            dst_ref=force_recv.at[src],
            send_sem=q_send.at[o],
            recv_sem=q_recv.at[src],
            device_id={"reps": lax.rem(rep + o, reps)},
            device_id_type=MESH,
        )

    for o in range(1, reps):
        force_copy(o, rep).start()

    for o in range(1, reps):
        for c in panel_copies(lax.rem(rep + o, reps), rep):
            c.wait_send()
    for s in range(rows):
        for o in range(1, cols):
            cross(s, o, False).wait_send()
            spread_col(s, o, lax.rem(row + s, rows), col).wait_send()
        if s < rows - 1:
            along(s, row).wait_send()
            spread_row(s + 1, row).wait_send()

    def energy_sent(q, carry):
        energy_copy(q, me).wait_send()
        return carry

    lax.fori_loop(1, total, energy_sent, 0)

    back = force_acc[rep]
    for o in range(1, reps):
        src = lax.rem(rep + o, reps)
        force_copy(o, src).wait_recv()
        back = back + force_recv[src]
    out_forces[...] = force_norm[0:3] - back[0:3]
    for o in range(1, reps):
        force_copy(o, rep).wait_send()


def local(
    scalars, vectors, positions, node_pose, source_block, target_block, block_count, shell_codes,
    weight_in, message_weight, filter_weights, read_scalar, read_vector, targets,
):
    rows, reps, cols = (lax.axis_size(name) for name in ("rows", "reps", "cols"))
    total = rows * reps * cols
    s_ch, blk = scalars.shape
    v_ch = vectors.shape[1]
    v3 = 3 * v_ch
    out_rows = s_ch + v3 + v_ch
    shells = filter_weights.shape[0]
    slots = shell_codes.shape[0]
    poses = targets.shape[0]
    pose_pad = -(-poses // 8) * 8
    width = shells * blk
    vmem = pl.BlockSpec(memory_space=pltpu.VMEM)
    smem = pl.BlockSpec(memory_space=pltpu.SMEM)
    anywhere = pl.BlockSpec(memory_space=pl.ANY)
    dma = pltpu.SemaphoreType.DMA
    new_scalars, new_vectors, scores, forces = pl.pallas_call(
        functools.partial(kernel, rows, reps, cols, poses, shells),
        out_shape=(
            jax.ShapeDtypeStruct((s_ch, blk), BF),
            jax.ShapeDtypeStruct((v3, blk), BF),
            jax.ShapeDtypeStruct((1, poses), F32),
            jax.ShapeDtypeStruct((3, blk), F32),
        ),
        in_specs=[vmem] * 4 + [smem] * 3 + [anywhere] + [vmem] * 5 + [smem],
        out_specs=(vmem,) * 4,
        scratch_shapes=[
            pltpu.VMEM((slots, blk, blk), jnp.int32),
            pltpu.VMEM((reps, s_ch, blk), BF),
            pltpu.VMEM((reps, v3, blk), BF),
            pltpu.VMEM((reps, 8, blk), F32),
            pltpu.VMEM((reps, v_ch, blk), F32),
            pltpu.VMEM((reps, out_rows, width), BF),
            pltpu.VMEM((s_ch + 2 * v_ch, width), F32),
            pltpu.VMEM((v_ch, blk), F32),
            pltpu.VMEM((rows, cols - 1, out_rows, blk), BF),
            pltpu.VMEM((rows, cols - 1, out_rows, blk), BF),
            pltpu.VMEM((rows, out_rows, blk), F32),
            pltpu.VMEM((rows, out_rows, blk), BF),
            pltpu.VMEM((rows, out_rows, blk), BF),
            pltpu.VMEM((v_ch, blk), F32),
            pltpu.VMEM((rows, cols, v3 + 16, blk), BF),
            pltpu.VMEM((total, pose_pad, blk), F32),
            pltpu.VMEM((reps, 8, blk), F32),
            pltpu.VMEM((reps, 8, blk), F32),
            pltpu.VMEM((8, blk), F32),
            dma,
            dma((3, reps)),
            dma((3, reps)),
            dma((rows, cols - 1)),
            dma((rows, cols - 1)),
            dma((rows,)),
            dma((rows,)),
            dma((rows,)),
            dma((rows, cols)),
            dma((rows, cols - 1)),
            dma((total,)),
            dma((total,)),
            dma((reps,)),
            dma((reps,)),
        ],
        compiler_params=pltpu.CompilerParams(
            collective_id=0, has_side_effects=True, vmem_limit_bytes=56 * 1024 * 1024
        ),
        name="layer",
    )(
        scalars, vectors.reshape(v3, blk), positions, node_pose.reshape(1, blk),
        source_block, target_block, block_count, shell_codes,
        weight_in, message_weight, filter_weights,
        read_scalar.reshape(1, s_ch), read_vector.reshape(1, v_ch), targets,
    )
    return (
        new_scalars, new_vectors.reshape(3, v_ch, blk), scores.reshape(poses), forces,
    )


def solution(mesh):
    spread = ("groups", "rows", "reps", "cols")
    placed = (
        P(None, spread),
        P(None, None, spread),
        P(None, spread),
        P(spread),
        P(spread),
        P(spread),
        P(spread),
        P(spread, None, None),
        P(),
        P(),
        P(),
        P(),
        P(),
        P("groups"),
    )
    return jax.shard_map(
        local,
        mesh=mesh,
        in_specs=placed,
        out_specs=(P(None, spread), P(None, None, spread), P("groups"), P(None, spread)),
        check_vma=False,
    )
```

```python
import functools

import jax
import jax.numpy as jnp
from jax import lax
from jax.experimental import pallas as pl
from jax.experimental.pallas import tpu as pltpu
from jax.sharding import PartitionSpec as P

POSE_ATOMS = 512
BF = jnp.bfloat16
F32 = jnp.float32
MESH = pl.DeviceIdType.MESH
HIGHEST = lax.Precision.HIGHEST


def kernel(
    rows, reps, cols, poses, shells,
    scalars, vectors, positions, node_pose, source_block, target_block, block_count, codes_hbm,
    weight_in, message_weight, filter_weights, read_scalar, read_vector, targets,
    out_scalars, out_vectors, out_scores, out_forces,
    codes, tables, sources, panel_s, panel_v, panel_p, gate_pos, rows_f, fwb, rv_col, xsend, xrecv, own, ssend, recv,
    norm_buf, gather, energies, force_acc, force_recv, force_norm,
    codes_sem, panel_send, panel_recv, x_send, x_recv, s_send, s_recv,
    g_send, g_recv, f_send, e_send, e_recv, q_send, q_recv,
):
    row = lax.axis_index("rows")
    rep = lax.axis_index("reps")
    col = lax.axis_index("cols")
    total = rows * reps * cols
    me = (row * reps + rep) * cols + col
    s_ch = scalars.shape[0]
    v3 = vectors.shape[0]
    v_ch = v3 // 3
    blk = scalars.shape[1]
    slots = codes.shape[0]
    places = rows * cols
    windows = -(-slots // places)
    pose_pad = -(-poses // 8) * 8

    def peer(q):
        flat = lax.rem(me + q, total)
        return flat, {
            "rows": flat // (reps * cols),
            "reps": lax.rem(flat // cols, reps),
            "cols": lax.rem(flat, cols),
        }

    barrier = pltpu.get_barrier_semaphore()

    def greet(q, carry):
        pl.semaphore_signal(barrier, inc=1, device_id=peer(q)[1], device_id_type=MESH)
        return carry

    lax.fori_loop(1, total, greet, 0)
    codes_copy = pltpu.make_async_copy(codes_hbm, codes, codes_sem)
    codes_copy.start()

    panel_p[rep] = jnp.zeros((8, blk), F32)
    panel_p[rep, 0:3, :] = positions[...].astype(F32)
    panel_s[rep] = scalars[...]
    panel_v[rep] = vectors[...]
    lane_shell = lax.broadcasted_iota(jnp.int32, (shells, shells * blk), 1) // blk
    sub_shell = lax.broadcasted_iota(jnp.int32, (shells, shells * blk), 0)
    spread = jnp.where(lane_shell == sub_shell, 1.0, 0.0).astype(BF)
    fwb[...] = lax.dot_general(
        filter_weights[...], spread, (((0,), (0,)), ((), ())), preferred_element_type=F32
    )
    rv_row = jnp.concatenate([read_vector[...], jnp.zeros((1, 128 - v_ch), F32)], axis=1)
    rv_col[...] = jnp.transpose(jnp.broadcast_to(rv_row, (blk, 128)))[:v_ch]

    pl.semaphore_wait(barrier, total - 1)

    def panel_copies(q, src_rep, which=(0, 1, 2)):
        out = []
        for a in which:
            buf = (panel_s, panel_v, panel_p)[a]
            out.append(
                pltpu.make_async_remote_copy(
                    src_ref=buf.at[src_rep],
                    dst_ref=buf.at[src_rep],
                    send_sem=panel_send.at[a, q],
                    recv_sem=panel_recv.at[a, src_rep],
                    device_id={"reps": q},
                    device_id_type=MESH,
                )
            )
        return out

    for o in range(1, reps):
        for c in panel_copies(lax.rem(rep + o, reps), rep):
            c.start()

    def make_rows(q, remote):
        if remote:
            panel_copies(q, q, (0,))[0].wait_recv()

        hidden = jnp.dot(weight_in[...], panel_s[q], preferred_element_type=F32)
        hidden = (hidden / (1.0 + jnp.exp(-hidden))).astype(BF)
        gates = jnp.dot(message_weight[...], hidden, preferred_element_type=F32).astype(BF)
        gates = gates.astype(F32)
        gs = gates[:s_ch]
        gv = gates[s_ch : s_ch + v_ch]
        gp = gates[s_ch + v_ch :]
        gate_pos[q] = gp
        if remote:
            for c in panel_copies(q, q, (1, 2)):
                c.wait_recv()

        pos = panel_p[q]
        vec = panel_v[q].astype(F32)
        gvv = [gv * vec[d * v_ch : (d + 1) * v_ch] for d in range(3)]
        gpp = [gp * pos[d : d + 1] for d in range(3)]
        for k in range(shells):
            span = pl.ds(k * blk, blk)
            rows_f[q, 1, :, span] = (gs * fwb[0:s_ch, span]).astype(BF)
            wv = fwb[s_ch : s_ch + v_ch, span]
            wp = fwb[s_ch + v_ch :, span]
            for d in range(3):
                rows_f[q, 0, d * v_ch : (d + 1) * v_ch, span] = (
                    gvv[d] * wv + gpp[d] * wp
                ).astype(BF)
            rows_f[q, 0, v3:, span] = (gp * wp).astype(BF)

    def find(dr, o, t):
        wanted = (lax.rem(row + dr, rows) * reps + rep) * cols + lax.rem(col + o, cols)
        slot = jnp.int32(0)
        found = jnp.int32(0)
        for e in range(t * places, min((t + 1) * places, slots)):
            hit = (target_block[e] == wanted) & (e < block_count[0])
            slot = jnp.where(hit, e, slot)
            found = jnp.where(hit, 1, found)
        return slot, found

    def table_step(dr, carry):
        for o in range(cols):
            for t in range(windows):
                slot, found = find(dr, o, t)
                sources[dr, o * windows + t] = lax.rem(source_block[slot] // cols, reps)
                code = codes[slot] * found
                for k in range(shells):
                    tables[dr, o * windows + t, k] = jnp.where(code == k + 1, 1.0, 0.0).astype(BF)
        return carry

    make_rows(rep, None)
    codes_copy.wait()
    lax.fori_loop(0, rows, table_step, 0)

    def rows_step(o, carry):
        make_rows(lax.rem(rep + o, reps), True)
        return carry

    lax.fori_loop(1, reps, rows_step, 0)

    def partial(h, dr, o):
        acc = None
        for t in range(windows):
            src = sources[dr, o * windows + t]
            table = tables[dr, o * windows + t].reshape(shells * blk, blk)
            term = jnp.dot(rows_f[src, h], table, preferred_element_type=F32)
            acc = term if acc is None else acc + term
        return acc

    def offset_of(u):
        s = lax.rem(u, rows)
        return jnp.where(s == rows - 1, 0, 1 + lax.rem(rows // 2 - 1 + s, rows - 1))

    def row_of(u):
        return lax.rem(row + offset_of(u), rows)

    def cross(s, o, arriving):
        if arriving:
            mine = o - 1
        else:
            mine = cols - o - 1
        return pltpu.make_async_remote_copy(
            src_ref=xsend.at[s, o - 1],
            dst_ref=xrecv.at[s, mine],
            send_sem=x_send.at[s, o - 1],
            recv_sem=x_recv.at[s, mine],
            device_id={"cols": lax.rem(col + o, cols)},
            device_id_type=MESH,
        )

    def along(u, src_row):
        h = u // rows
        return pltpu.make_async_remote_copy(
            src_ref=ssend.at[u],
            dst_ref=recv.at[h, src_row],
            send_sem=s_send.at[u],
            recv_sem=s_recv.at[h, src_row],
            device_id={"rows": row_of(u)},
            device_id_type=MESH,
        )

    def finish(u):
        for o in range(1, cols):
            cross(u, o, True).wait_recv()
        both = own[u]
        for o in range(1, cols):
            both = both + xrecv[u, o - 1].astype(F32)
        return both

    def forward_step(u, carry):
        h = u // rows
        dr = offset_of(u)
        for o in range(1, cols):
            xsend[u, o - 1] = partial(h, dr, o).astype(BF)
            cross(u, o, False).start()

        own[u] = partial(h, dr, 0)

        @pl.when(lax.rem(u, rows) < rows - 1)
        def _():
            ssend[u] = finish(u).astype(BF)
            along(u, row).start()

        return carry

    lax.fori_loop(0, 2 * rows, forward_step, 0)

    def arrive(h):
        own[h * rows + rows - 1] = finish(h * rows + rows - 1)
        for u in range(h * rows, h * rows + rows - 1):
            along(u, row_of(u)).wait_recv()

    def message(h, lo, hi):
        acc = own[h * rows + rows - 1, lo:hi]
        for s in range(rows - 1):
            acc = acc + recv[h, row_of(s), lo:hi].astype(F32)
        return acc

    arrive(0)
    norm = message(0, v3, v3 + v_ch)
    norm_buf[...] = norm
    pos_own = panel_p[rep]
    square = jnp.zeros((v_ch, blk), F32)
    for d in range(3):
        lo = d * v_ch
        nv = (
            vectors[lo : lo + v_ch].astype(F32)
            + message(0, lo, lo + v_ch)
            - pos_own[d : d + 1] * norm
        ).astype(BF)
        out_vectors[lo : lo + v_ch] = nv
        gather[row, col, lo : lo + v_ch] = nv
        nv = nv.astype(F32)
        square = square + nv * nv
    pose_row = node_pose[...]
    gather[row, col, v3 : v3 + 16] = jnp.broadcast_to(pose_row.astype(F32), (16, blk)).astype(BF)

    def spread_row(o, src_row):
        return pltpu.make_async_remote_copy(
            src_ref=gather.at[src_row, col],
            dst_ref=gather.at[src_row, col],
            send_sem=g_send.at[o],
            recv_sem=g_recv.at[src_row, col],
            device_id={"rows": lax.rem(row + o, rows)},
            device_id_type=MESH,
        )

    def spread_col(s, o, src_row, src_col):
        return pltpu.make_async_remote_copy(
            src_ref=gather.at[src_row, src_col],
            dst_ref=gather.at[src_row, src_col],
            send_sem=f_send.at[s, o - 1],
            recv_sem=g_recv.at[src_row, src_col],
            device_id={"cols": lax.rem(col + o, cols)},
            device_id_type=MESH,
        )

    for i in range(rows - 1):
        o = 1 + (rows // 2 - 1 + i) % (rows - 1)
        spread_row(o, row).start()
    for o in range(1, cols):
        spread_col(0, o, row, col).start()

    arrive(1)
    ns = (scalars[...].astype(F32) + message(1, 0, s_ch)).astype(BF)
    out_scalars[...] = ns
    energy = jnp.dot(
        read_scalar[...], ns.astype(F32), preferred_element_type=F32, precision=HIGHEST
    ) + jnp.dot(read_vector[...], square, preferred_element_type=F32, precision=HIGHEST)
    pose_iota = lax.broadcasted_iota(jnp.int32, (pose_pad, blk), 0)
    lane_iota = lax.broadcasted_iota(jnp.int32, (pose_pad, blk), 1)
    by_pose = jnp.sum(
        jnp.where(
            jnp.broadcast_to(pose_row, (pose_pad, blk)) == pose_iota,
            jnp.broadcast_to(energy, (pose_pad, blk)),
            0.0,
        ),
        axis=1,
        keepdims=True,
    )
    energies[me] = jnp.sum(
        jnp.where(lane_iota == pose_iota, jnp.broadcast_to(by_pose, (pose_pad, blk)), 0.0),
        axis=0,
        keepdims=True,
    )

    def energy_copy(q, src):
        return pltpu.make_async_remote_copy(
            src_ref=energies.at[src],
            dst_ref=energies.at[src],
            send_sem=e_send.at[q],
            recv_sem=e_recv.at[src],
            device_id=peer(q)[1],
            device_id_type=MESH,
        )

    def energy_start(q, carry):
        energy_copy(q, me).start()
        return carry

    def energy_wait(q, carry):
        energy_copy(q, peer(q)[0]).wait_recv()
        return carry

    lax.fori_loop(1, total, energy_start, 0)
    force_acc[...] = jnp.zeros_like(force_acc)
    for s in range(1, rows):
        r = lax.rem(row + s, rows)
        spread_row(1, r).wait_recv()
        for o in range(1, cols):
            spread_col(s, o, r, col).start()
    lax.fori_loop(1, total, energy_wait, 0)
    sums = energies[0]
    for q in range(1, total):
        sums = sums + energies[q]
    score_row = sums / POSE_ATOMS
    out_scores[...] = score_row[:, :poses]
    scores = jnp.broadcast_to(
        jnp.sum(
            jnp.where(
                lane_iota == pose_iota, jnp.broadcast_to(score_row, (pose_pad, blk)), 0.0
            ),
            axis=1,
            keepdims=True,
        ),
        (pose_pad, blk),
    )
    wanted = jnp.zeros((pose_pad, blk), F32)
    for p in range(poses):
        wanted = jnp.where(pose_iota == p, targets[p], wanted)
    resid = scores - wanted

    def gradient(r, c):
        pose = gather[r, c, v3 : v3 + 16].astype(F32)[0:1]
        member = jnp.broadcast_to(pose, (pose_pad, blk)) == pose_iota.astype(F32)
        node_resid = jnp.sum(jnp.where(member, resid, 0.0), axis=0, keepdims=True)
        scale = 2.0 * node_resid * rv_col[...]
        return [
            (scale * gather[r, c, d * v_ch : (d + 1) * v_ch].astype(F32)).astype(BF).astype(F32)
            for d in range(3)
        ]

    own_grad = gradient(row, col)
    for d in range(3):
        force_norm[d : d + 1] = jnp.sum(norm_buf[...] * own_grad[d], axis=0, keepdims=True)

    def backward(s, o):
        r, c = lax.rem(row + s, rows), lax.rem(col + o, cols)
        grad = gradient(r, c)
        weights = [fwb[s_ch + v_ch :, k * blk : (k + 1) * blk] for k in range(shells)]
        left = jnp.concatenate(
            [
                jnp.concatenate([(grad[d] * w).astype(BF) for w in weights], axis=1)
                for d in range(3)
            ],
            axis=0,
        )
        table = jnp.concatenate(
            [
                jnp.concatenate([tables[s, o * windows + t, k] for k in range(shells)], axis=1)
                for t in range(windows)
            ],
            axis=0,
        )
        back = lax.dot_general(
            left, table, (((1,), (1,)), ((), ())), preferred_element_type=F32
        )
        for t in range(windows):
            src = sources[s, o * windows + t]
            gp = gate_pos[src]
            for d in range(3):
                piece = back[d * v_ch : (d + 1) * v_ch, t * blk : (t + 1) * blk]
                term = jnp.sum(gp * piece, axis=0, keepdims=True)
                for q in range(reps):
                    force_acc[q, d : d + 1] += jnp.where(src == q, term, 0.0)

    def backward_step(s, carry):
        r = lax.rem(row + s, rows)

        backward(s, 0)
        for o in range(1, cols):
            c = lax.rem(col + o, cols)
            spread_col(s, o, r, c).wait_recv()
            backward(s, o)
        return carry

    lax.fori_loop(0, rows, backward_step, 0)

    def force_copy(o, src):
        return pltpu.make_async_remote_copy(
            src_ref=force_acc.at[lax.rem(rep + o, reps)],
            dst_ref=force_recv.at[src],
            send_sem=q_send.at[o],
            recv_sem=q_recv.at[src],
            device_id={"reps": lax.rem(rep + o, reps)},
            device_id_type=MESH,
        )

    for o in range(1, reps):
        force_copy(o, rep).start()

    for o in range(1, reps):
        for c in panel_copies(lax.rem(rep + o, reps), rep):
            c.wait_send()
    for s in range(rows):
        for o in range(1, cols):
            spread_col(s, o, lax.rem(row + s, rows), col).wait_send()
        if s < rows - 1:
            spread_row(s + 1, row).wait_send()

    for u in range(2 * rows):
        for o in range(1, cols):
            cross(u, o, False).wait_send()
        if u % rows < rows - 1:
            along(u, row).wait_send()

    def energy_sent(q, carry):
        energy_copy(q, me).wait_send()
        return carry

    lax.fori_loop(1, total, energy_sent, 0)

    back = force_acc[rep]
    for o in range(1, reps):
        src = lax.rem(rep + o, reps)
        force_copy(o, src).wait_recv()
        back = back + force_recv[src]
    out_forces[...] = force_norm[0:3] - back[0:3]
    for o in range(1, reps):
        force_copy(o, rep).wait_send()


def publish(*refs):
    count = len(refs) // 2
    for source, target in zip(refs[:count], refs[count:]):
        target[...] = source[...]


def local(
    scalars, vectors, positions, node_pose, source_block, target_block, block_count, shell_codes,
    weight_in, message_weight, filter_weights, read_scalar, read_vector, targets,
):
    rows, reps, cols = (lax.axis_size(name) for name in ("rows", "reps", "cols"))
    total = rows * reps * cols
    s_ch, blk = scalars.shape
    v_ch = vectors.shape[1]
    v3 = 3 * v_ch
    half = s_ch
    shells = filter_weights.shape[0]
    slots = shell_codes.shape[0]
    poses = targets.shape[0]
    windows = -(-slots // (rows * cols))
    width = shells * blk
    vmem = pl.BlockSpec(memory_space=pltpu.VMEM)
    smem = pl.BlockSpec(memory_space=pltpu.SMEM)
    anywhere = pl.BlockSpec(memory_space=pl.ANY)
    dma = pltpu.SemaphoreType.DMA
    results = pl.pallas_call(
        functools.partial(kernel, rows, reps, cols, poses, shells),
        out_shape=(
            jax.ShapeDtypeStruct((s_ch, blk), BF),
            jax.ShapeDtypeStruct((v3, blk), BF),
            jax.ShapeDtypeStruct((1, poses), F32),
            jax.ShapeDtypeStruct((3, blk), F32),
        ),
        in_specs=[vmem] * 4 + [smem] * 3 + [anywhere] + [vmem] * 5 + [smem],
        out_specs=(vmem,) * 4,
        scratch_shapes=[
            pltpu.VMEM((slots, blk, blk), jnp.int32),
            pltpu.VMEM((rows, cols * windows, shells, blk, blk), BF),
            pltpu.SMEM((rows, cols * windows), jnp.int32),
            pltpu.VMEM((reps, s_ch, blk), BF),
            pltpu.VMEM((reps, v3, blk), BF),
            pltpu.VMEM((reps, 8, blk), F32),
            pltpu.VMEM((reps, v_ch, blk), F32),
            pltpu.VMEM((reps, 2, half, width), BF),
            pltpu.VMEM((s_ch + 2 * v_ch, width), F32),
            pltpu.VMEM((v_ch, blk), F32),
            pltpu.VMEM((2 * rows, cols - 1, half, blk), BF),
            pltpu.VMEM((2 * rows, cols - 1, half, blk), BF),
            pltpu.VMEM((2 * rows, half, blk), F32),
            pltpu.VMEM((2 * rows, half, blk), BF),
            pltpu.VMEM((2, rows, half, blk), BF),
            pltpu.VMEM((v_ch, blk), F32),
            pltpu.VMEM((rows, cols, v3 + 16, blk), BF),
            pltpu.VMEM((total, 1, blk), F32),
            pltpu.VMEM((reps, 8, blk), F32),
            pltpu.VMEM((reps, 8, blk), F32),
            pltpu.VMEM((8, blk), F32),
            dma,
            dma((3, reps)),
            dma((3, reps)),
            dma((2 * rows, cols - 1)),
            dma((2 * rows, cols - 1)),
            dma((2 * rows,)),
            dma((2, rows)),
            dma((rows,)),
            dma((rows, cols)),
            dma((rows, cols - 1)),
            dma((total,)),
            dma((total,)),
            dma((reps,)),
            dma((reps,)),
        ],
        compiler_params=pltpu.CompilerParams(
            collective_id=0, has_side_effects=True, vmem_limit_bytes=56 * 1024 * 1024
        ),
        name="layer",
    )(
        scalars, vectors.reshape(v3, blk), positions, node_pose.reshape(1, blk),
        source_block, target_block, block_count, shell_codes,
        weight_in, message_weight, filter_weights,
        read_scalar.reshape(1, s_ch), read_vector.reshape(1, v_ch), targets,
    )
    new_scalars, new_vectors, scores, forces = pl.pallas_call(
        publish,
        out_shape=tuple(jax.ShapeDtypeStruct(x.shape, x.dtype) for x in results),
        in_specs=[vmem] * 4,
        out_specs=(vmem,) * 4,
        name="publish",
    )(*results)
    return (
        new_scalars, new_vectors.reshape(3, v_ch, blk), scores.reshape(poses), forces,
    )


def solution(mesh):
    spread = ("groups", "rows", "reps", "cols")
    placed = (
        P(None, spread),
        P(None, None, spread),
        P(None, spread),
        P(spread),
        P(spread),
        P(spread),
        P(spread),
        P(spread, None, None),
        P(),
        P(),
        P(),
        P(),
        P(),
        P("groups"),
    )
    return jax.shard_map(
        local,
        mesh=mesh,
        in_specs=placed,
        out_specs=(P(None, spread), P(None, None, spread), P("groups"), P(None, spread)),
        check_vma=False,
    )
```

```python
import functools

import jax
import jax.numpy as jnp
from jax import lax
from jax.experimental import pallas as pl
from jax.experimental.pallas import tpu as pltpu
from jax.sharding import PartitionSpec as P

POSE_ATOMS = 512
BF = jnp.bfloat16
F32 = jnp.float32
MESH = pl.DeviceIdType.MESH


def kernel(
    rows, reps, cols, poses, shells,
    scalars, vectors, positions, node_pose, source_block, target_block, block_count, codes_hbm,
    weight_in, message_weight, filter_weights, read_scalar, read_vector, targets,
    out_scalars, out_vectors, out_scores, out_forces,
    codes, tables, turned, sources, picked, live, panel_s, panel_v, panel_p, gate_pos, rows_f, fwb, rv_col, rs_col, xsend, xrecv, own, ssend, recv,
    norm_buf, gather, energies, force_acc, force_recv, force_norm,
    codes_sem, panel_send, panel_recv, x_send, x_recv, s_send, s_recv,
    g_send, g_recv, f_send, e_send, e_recv, q_send, q_recv,
):
    row = lax.axis_index("rows")
    rep = lax.axis_index("reps")
    col = lax.axis_index("cols")
    total = rows * reps * cols
    me = (row * reps + rep) * cols + col
    s_ch = scalars.shape[0]
    v3 = vectors.shape[0]
    v_ch = v3 // 3
    blk = scalars.shape[1]
    slots = codes.shape[0]
    places = rows * cols
    windows = -(-slots // places)
    pose_pad = -(-poses // 8) * 8

    def peer(q):
        flat = lax.rem(me + q, total)
        return flat, {
            "rows": flat // (reps * cols),
            "reps": lax.rem(flat // cols, reps),
            "cols": lax.rem(flat, cols),
        }

    barrier = pltpu.get_barrier_semaphore()

    def greet(q, carry):
        pl.semaphore_signal(barrier, inc=1, device_id=peer(q)[1], device_id_type=MESH)
        return carry

    lax.fori_loop(1, total, greet, 0)
    codes_copy = pltpu.make_async_copy(codes_hbm, codes, codes_sem)
    codes_copy.start()

    panel_p[rep] = jnp.zeros((8, blk), F32)
    panel_p[rep, 0:3, :] = positions[...].astype(F32)
    panel_s[rep] = scalars[...]
    panel_v[rep] = vectors[...]
    lane_shell = lax.broadcasted_iota(jnp.int32, (shells, shells * blk), 1) // blk
    sub_shell = lax.broadcasted_iota(jnp.int32, (shells, shells * blk), 0)
    spread = jnp.where(lane_shell == sub_shell, 1.0, 0.0).astype(BF)
    fwb[...] = lax.dot_general(
        filter_weights[...], spread, (((0,), (0,)), ((), ())), preferred_element_type=F32
    )
    rv_row = jnp.concatenate([read_vector[...], jnp.zeros((1, 128 - v_ch), F32)], axis=1)
    rv_col[...] = jnp.transpose(jnp.broadcast_to(rv_row, (blk, 128)))[:v_ch]

    rs_col[...] = jnp.transpose(jnp.broadcast_to(read_scalar[...], (blk, s_ch)))

    pl.semaphore_wait(barrier, total - 1)

    def panel_copies(q, src_rep, which=(0, 1, 2)):
        out = []
        for a in which:
            buf = (panel_s, panel_v, panel_p)[a]
            out.append(
                pltpu.make_async_remote_copy(
                    src_ref=buf.at[src_rep],
                    dst_ref=buf.at[src_rep],
                    send_sem=panel_send.at[a, q],
                    recv_sem=panel_recv.at[a, src_rep],
                    device_id={"reps": q},
                    device_id_type=MESH,
                )
            )
        return out

    for o in range(1, reps):
        for c in panel_copies(lax.rem(rep + o, reps), rep):
            c.start()

    def make_rows(q, remote):
        if remote:
            panel_copies(q, q, (0,))[0].wait_recv()

        hidden = jnp.dot(weight_in[...], panel_s[q], preferred_element_type=F32)
        hidden = (hidden / (1.0 + jnp.exp(-hidden))).astype(BF)
        gates = jnp.dot(message_weight[...], hidden, preferred_element_type=F32).astype(BF)
        gates = gates.astype(F32)
        gs = gates[:s_ch]
        gv = gates[s_ch : s_ch + v_ch]
        gp = gates[s_ch + v_ch :]
        gate_pos[q] = gp
        if remote:
            for c in panel_copies(q, q, (1, 2)):
                c.wait_recv()

        pos = panel_p[q]
        vec = panel_v[q].astype(F32)
        gvv = [gv * vec[d * v_ch : (d + 1) * v_ch] for d in range(3)]
        gpp = [gp * pos[d : d + 1] for d in range(3)]
        for k in range(shells):
            span = pl.ds(k * blk, blk)
            rows_f[q, 1, :, span] = (gs * fwb[0:s_ch, span]).astype(BF)
            wv = fwb[s_ch : s_ch + v_ch, span]
            wp = fwb[s_ch + v_ch :, span]
            for d in range(3):
                rows_f[q, 0, d * v_ch : (d + 1) * v_ch, span] = (
                    gvv[d] * wv + gpp[d] * wp
                ).astype(BF)
            rows_f[q, 0, v3:, span] = (gp * wp).astype(BF)

    def find(dr, o, t):
        wanted = (lax.rem(row + dr, rows) * reps + rep) * cols + lax.rem(col + o, cols)
        slot = jnp.int32(0)
        found = jnp.int32(0)
        for e in range(t * places, min((t + 1) * places, slots)):
            hit = (target_block[e] == wanted) & (e < block_count[0])
            slot = jnp.where(hit, e, slot)
            found = jnp.where(hit, 1, found)
        return slot, found

    def table_step(dr, carry):
        for o in range(cols):
            for t in range(windows):
                slot, found = find(dr, o, t)
                sources[dr, o * windows + t] = lax.rem(source_block[slot] // cols, reps)
                picked[dr, o * windows + t] = slot
                live[dr, o * windows + t] = found
                code = codes[slot] * found
                for k in range(shells):
                    tables[dr, o * windows + t, k] = jnp.where(code == k + 1, 1.0, 0.0).astype(BF)
        return carry

    def turn_step(dr, carry):
        for o in range(cols):
            for t in range(windows):
                code = codes[picked[dr, o * windows + t]] * live[dr, o * windows + t]
                code = jnp.transpose(code.astype(F32))
                for k in range(shells):
                    turned[dr, o, k, :, t * blk : (t + 1) * blk] = jnp.where(
                        code == float(k + 1), 1.0, 0.0
                    ).astype(BF)
        return carry

    make_rows(rep, None)
    codes_copy.wait()
    lax.fori_loop(0, rows, table_step, 0)

    def rows_step(o, carry):
        make_rows(lax.rem(rep + o, reps), True)
        return carry

    lax.fori_loop(1, reps, rows_step, 0)

    def partial(h, dr, o):
        acc = None
        for t in range(windows):
            src = sources[dr, o * windows + t]
            table = tables[dr, o * windows + t].reshape(shells * blk, blk)
            term = jnp.dot(rows_f[src, h], table, preferred_element_type=F32)
            acc = term if acc is None else acc + term
        return acc

    def offset_of(u):
        s = lax.rem(u, rows)
        return jnp.where(s == rows - 1, 0, 1 + lax.rem(rows // 2 - 1 + s, rows - 1))

    def row_of(u):
        return lax.rem(row + offset_of(u), rows)

    def cross(s, o, arriving):
        if arriving:
            mine = o - 1
        else:
            mine = cols - o - 1
        return pltpu.make_async_remote_copy(
            src_ref=xsend.at[s, o - 1],
            dst_ref=xrecv.at[s, mine],
            send_sem=x_send.at[s, o - 1],
            recv_sem=x_recv.at[s, mine],
            device_id={"cols": lax.rem(col + o, cols)},
            device_id_type=MESH,
        )

    def along(u, src_row):
        h = u // rows
        return pltpu.make_async_remote_copy(
            src_ref=ssend.at[u],
            dst_ref=recv.at[h, src_row],
            send_sem=s_send.at[u],
            recv_sem=s_recv.at[h, src_row],
            device_id={"rows": row_of(u)},
            device_id_type=MESH,
        )

    def finish(u):
        for o in range(1, cols):
            cross(u, o, True).wait_recv()
        both = own[u]
        for o in range(1, cols):
            both = both + xrecv[u, o - 1].astype(F32)
        return both

    ahead = min(2, 2 * rows)

    def cross_step(u, carry):
        for o in range(1, cols):
            xsend[u, o - 1] = partial(u // rows, offset_of(u), o).astype(BF)
            cross(u, o, False).start()
        return carry

    def forward_step(u, carry):
        @pl.when(u + ahead < 2 * rows)
        def _():
            cross_step(u + ahead, 0)

        own[u] = partial(u // rows, offset_of(u), 0)

        @pl.when(lax.rem(u, rows) < rows - 1)
        def _():
            ssend[u] = finish(u).astype(BF)
            along(u, row).start()

        return carry

    lax.fori_loop(0, ahead, cross_step, 0)
    lax.fori_loop(0, 2 * rows, forward_step, 0)
    lax.fori_loop(0, rows, turn_step, 0)

    def arrive(h):
        own[h * rows + rows - 1] = finish(h * rows + rows - 1)
        for u in range(h * rows, h * rows + rows - 1):
            along(u, row_of(u)).wait_recv()

    def message(h, lo, hi):
        acc = own[h * rows + rows - 1, lo:hi]
        for s in range(rows - 1):
            acc = acc + recv[h, row_of(s), lo:hi].astype(F32)
        return acc

    arrive(0)
    norm = message(0, v3, v3 + v_ch)
    norm_buf[...] = norm
    pos_own = panel_p[rep]
    square = jnp.zeros((v_ch, blk), F32)
    for d in range(3):
        lo = d * v_ch
        nv = (
            vectors[lo : lo + v_ch].astype(F32)
            + message(0, lo, lo + v_ch)
            - pos_own[d : d + 1] * norm
        ).astype(BF)
        out_vectors[lo : lo + v_ch] = nv
        gather[row, col, lo : lo + v_ch] = nv
        nv = nv.astype(F32)
        square = square + nv * nv
    pose_row = node_pose[...]
    gather[row, col, v3 : v3 + 16] = jnp.broadcast_to(pose_row.astype(F32), (16, blk)).astype(BF)

    def spread_row(o, src_row):
        return pltpu.make_async_remote_copy(
            src_ref=gather.at[src_row, col],
            dst_ref=gather.at[src_row, col],
            send_sem=g_send.at[o],
            recv_sem=g_recv.at[src_row, col],
            device_id={"rows": lax.rem(row + o, rows)},
            device_id_type=MESH,
        )

    def spread_col(s, o, src_row, src_col):
        return pltpu.make_async_remote_copy(
            src_ref=gather.at[src_row, src_col],
            dst_ref=gather.at[src_row, src_col],
            send_sem=f_send.at[s, o - 1],
            recv_sem=g_recv.at[src_row, src_col],
            device_id={"cols": lax.rem(col + o, cols)},
            device_id_type=MESH,
        )

    for i in range(rows - 1):
        o = 1 + (rows // 2 - 1 + i) % (rows - 1)
        spread_row(o, row).start()
    for o in range(1, cols):
        spread_col(0, o, row, col).start()

    vector_energy = jnp.sum(rv_col[...] * square, axis=0, keepdims=True)
    arrive(1)
    ns = (scalars[...].astype(F32) + message(1, 0, s_ch)).astype(BF)
    out_scalars[...] = ns
    energy = vector_energy + jnp.sum(rs_col[...] * ns.astype(F32), axis=0, keepdims=True)
    pose_iota = lax.broadcasted_iota(jnp.int32, (pose_pad, blk), 0)
    lane_iota = lax.broadcasted_iota(jnp.int32, (pose_pad, blk), 1)
    by_pose = jnp.sum(
        jnp.where(
            jnp.broadcast_to(pose_row, (pose_pad, blk)) == pose_iota,
            jnp.broadcast_to(energy, (pose_pad, blk)),
            0.0,
        ),
        axis=1,
        keepdims=True,
    )
    energies[me] = jnp.sum(
        jnp.where(lane_iota == pose_iota, jnp.broadcast_to(by_pose, (pose_pad, blk)), 0.0),
        axis=0,
        keepdims=True,
    )

    def energy_copy(q, src):
        return pltpu.make_async_remote_copy(
            src_ref=energies.at[src],
            dst_ref=energies.at[src],
            send_sem=e_send.at[q],
            recv_sem=e_recv.at[src],
            device_id=peer(q)[1],
            device_id_type=MESH,
        )

    def energy_start(q, carry):
        energy_copy(q, me).start()
        return carry

    def energy_wait(q, carry):
        energy_copy(q, peer(q)[0]).wait_recv()
        return carry

    lax.fori_loop(1, total, energy_start, 0)
    force_acc[...] = jnp.zeros_like(force_acc)
    for s in range(1, rows):
        r = lax.rem(row + s, rows)
        spread_row(1, r).wait_recv()
        for o in range(1, cols):
            spread_col(s, o, r, col).start()
    for s in range(rows):
        for o in range(1, cols):
            spread_col(s, o, lax.rem(row + s, rows), lax.rem(col + o, cols)).wait_recv()
    lax.fori_loop(1, total, energy_wait, 0)
    sums = energies[0]
    for q in range(1, total):
        sums = sums + energies[q]
    score_row = sums / POSE_ATOMS
    out_scores[...] = score_row[:, :poses]
    scores = jnp.broadcast_to(
        jnp.sum(
            jnp.where(
                lane_iota == pose_iota, jnp.broadcast_to(score_row, (pose_pad, blk)), 0.0
            ),
            axis=1,
            keepdims=True,
        ),
        (pose_pad, blk),
    )
    wanted = jnp.zeros((pose_pad, blk), F32)
    for p in range(poses):
        wanted = jnp.where(pose_iota == p, targets[p], wanted)
    resid = scores - wanted

    def gradient(r, c):
        pose = gather[r, c, v3 : v3 + 16].astype(F32)[0:1]
        member = jnp.broadcast_to(pose, (pose_pad, blk)) == pose_iota.astype(F32)
        node_resid = jnp.sum(jnp.where(member, resid, 0.0), axis=0, keepdims=True)
        scale = 2.0 * node_resid * rv_col[...]
        return [
            (scale * gather[r, c, d * v_ch : (d + 1) * v_ch].astype(F32)).astype(BF).astype(F32)
            for d in range(3)
        ]

    own_grad = gradient(row, col)
    for d in range(3):
        force_norm[d : d + 1] = jnp.sum(norm_buf[...] * own_grad[d], axis=0, keepdims=True)

    def backward(s, o):
        r, c = lax.rem(row + s, rows), lax.rem(col + o, cols)
        grad = gradient(r, c)
        weights = [fwb[s_ch + v_ch :, k * blk : (k + 1) * blk] for k in range(shells)]
        left = jnp.concatenate(
            [
                jnp.concatenate([(grad[d] * w).astype(BF) for w in weights], axis=1)
                for d in range(3)
            ],
            axis=0,
        )
        table = turned[s, o].reshape(shells * blk, windows * blk)
        back = jnp.dot(left, table, preferred_element_type=F32)
        for t in range(windows):
            src = sources[s, o * windows + t]
            gp = gate_pos[src]
            for d in range(3):
                piece = back[d * v_ch : (d + 1) * v_ch, t * blk : (t + 1) * blk]
                term = jnp.sum(gp * piece, axis=0, keepdims=True)
                for q in range(reps):
                    force_acc[q, d : d + 1] += jnp.where(src == q, term, 0.0)

    def backward_step(s, carry):
        for o in range(cols):
            backward(s, o)
        return carry

    lax.fori_loop(0, rows, backward_step, 0, unroll=2 if rows % 2 == 0 else 1)

    def force_copy(o, src):
        return pltpu.make_async_remote_copy(
            src_ref=force_acc.at[lax.rem(rep + o, reps)],
            dst_ref=force_recv.at[src],
            send_sem=q_send.at[o],
            recv_sem=q_recv.at[src],
            device_id={"reps": lax.rem(rep + o, reps)},
            device_id_type=MESH,
        )

    for o in range(1, reps):
        force_copy(o, rep).start()

    for o in range(1, reps):
        for c in panel_copies(lax.rem(rep + o, reps), rep):
            c.wait_send()
    for s in range(rows):
        for o in range(1, cols):
            spread_col(s, o, lax.rem(row + s, rows), col).wait_send()
        if s < rows - 1:
            spread_row(s + 1, row).wait_send()

    for u in range(2 * rows):
        for o in range(1, cols):
            cross(u, o, False).wait_send()
        if u % rows < rows - 1:
            along(u, row).wait_send()

    def energy_sent(q, carry):
        energy_copy(q, me).wait_send()
        return carry

    lax.fori_loop(1, total, energy_sent, 0)

    back = force_acc[rep]
    for o in range(1, reps):
        src = lax.rem(rep + o, reps)
        force_copy(o, src).wait_recv()
        back = back + force_recv[src]
    out_forces[...] = force_norm[0:3] - back[0:3]
    for o in range(1, reps):
        force_copy(o, rep).wait_send()


def publish(*refs):
    count = len(refs) // 2
    for source, target in zip(refs[:count], refs[count:]):
        target[...] = source[...]


def local(
    scalars, vectors, positions, node_pose, source_block, target_block, block_count, shell_codes,
    weight_in, message_weight, filter_weights, read_scalar, read_vector, targets,
):
    rows, reps, cols = (lax.axis_size(name) for name in ("rows", "reps", "cols"))
    total = rows * reps * cols
    s_ch, blk = scalars.shape
    v_ch = vectors.shape[1]
    v3 = 3 * v_ch
    half = s_ch
    shells = filter_weights.shape[0]
    slots = shell_codes.shape[0]
    poses = targets.shape[0]
    windows = -(-slots // (rows * cols))
    width = shells * blk
    vmem = pl.BlockSpec(memory_space=pltpu.VMEM)
    smem = pl.BlockSpec(memory_space=pltpu.SMEM)
    anywhere = pl.BlockSpec(memory_space=pl.ANY)
    dma = pltpu.SemaphoreType.DMA
    results = pl.pallas_call(
        functools.partial(kernel, rows, reps, cols, poses, shells),
        out_shape=(
            jax.ShapeDtypeStruct((s_ch, blk), BF),
            jax.ShapeDtypeStruct((v3, blk), BF),
            jax.ShapeDtypeStruct((1, poses), F32),
            jax.ShapeDtypeStruct((3, blk), F32),
        ),
        in_specs=[vmem] * 4 + [smem] * 3 + [anywhere] + [vmem] * 5 + [smem],
        out_specs=(vmem,) * 4,
        scratch_shapes=[
            pltpu.VMEM((slots, blk, blk), jnp.int32),
            pltpu.VMEM((rows, cols * windows, shells, blk, blk), BF),
            pltpu.VMEM((rows, cols, shells, blk, windows * blk), BF),
            pltpu.SMEM((rows, cols * windows), jnp.int32),
            pltpu.SMEM((rows, cols * windows), jnp.int32),
            pltpu.SMEM((rows, cols * windows), jnp.int32),
            pltpu.VMEM((reps, s_ch, blk), BF),
            pltpu.VMEM((reps, v3, blk), BF),
            pltpu.VMEM((reps, 8, blk), F32),
            pltpu.VMEM((reps, v_ch, blk), F32),
            pltpu.VMEM((reps, 2, half, width), BF),
            pltpu.VMEM((s_ch + 2 * v_ch, width), F32),
            pltpu.VMEM((v_ch, blk), F32),
            pltpu.VMEM((s_ch, blk), F32),
            pltpu.VMEM((2 * rows, cols - 1, half, blk), BF),
            pltpu.VMEM((2 * rows, cols - 1, half, blk), BF),
            pltpu.VMEM((2 * rows, half, blk), F32),
            pltpu.VMEM((2 * rows, half, blk), BF),
            pltpu.VMEM((2, rows, half, blk), BF),
            pltpu.VMEM((v_ch, blk), F32),
            pltpu.VMEM((rows, cols, v3 + 16, blk), BF),
            pltpu.VMEM((total, 1, blk), F32),
            pltpu.VMEM((reps, 8, blk), F32),
            pltpu.VMEM((reps, 8, blk), F32),
            pltpu.VMEM((8, blk), F32),
            dma,
            dma((3, reps)),
            dma((3, reps)),
            dma((2 * rows, cols - 1)),
            dma((2 * rows, cols - 1)),
            dma((2 * rows,)),
            dma((2, rows)),
            dma((rows,)),
            dma((rows, cols)),
            dma((rows, cols - 1)),
            dma((total,)),
            dma((total,)),
            dma((reps,)),
            dma((reps,)),
        ],
        compiler_params=pltpu.CompilerParams(
            collective_id=0, has_side_effects=True, vmem_limit_bytes=56 * 1024 * 1024
        ),
        name="layer",
    )(
        scalars, vectors.reshape(v3, blk), positions, node_pose.reshape(1, blk),
        source_block, target_block, block_count, shell_codes,
        weight_in, message_weight, filter_weights,
        read_scalar.reshape(1, s_ch), read_vector.reshape(1, v_ch), targets,
    )
    new_scalars, new_vectors, scores, forces = pl.pallas_call(
        publish,
        out_shape=tuple(jax.ShapeDtypeStruct(x.shape, x.dtype) for x in results),
        in_specs=[vmem] * 4,
        out_specs=(vmem,) * 4,
        name="publish",
    )(*results)
    return (
        new_scalars, new_vectors.reshape(3, v_ch, blk), scores.reshape(poses), forces,
    )


def solution(mesh):
    spread = ("groups", "rows", "reps", "cols")
    placed = (
        P(None, spread),
        P(None, None, spread),
        P(None, spread),
        P(spread),
        P(spread),
        P(spread),
        P(spread),
        P(spread, None, None),
        P(),
        P(),
        P(),
        P(),
        P(),
        P("groups"),
    )
    return jax.shard_map(
        local,
        mesh=mesh,
        in_specs=placed,
        out_specs=(P(None, spread), P(None, None, spread), P("groups"), P(None, spread)),
        check_vma=False,
    )
```

```python
import functools

import jax
import jax.numpy as jnp
from jax import lax
from jax.experimental import pallas as pl
from jax.experimental.pallas import tpu as pltpu
from jax.sharding import PartitionSpec as P

POSE_ATOMS = 512
BF = jnp.bfloat16
F32 = jnp.float32
MESH = pl.DeviceIdType.MESH


def kernel(
    rows, reps, cols, poses, shells,
    scalars, vectors, positions, node_pose, source_block, target_block, block_count, codes_hbm,
    weight_in, message_weight, filter_weights, read_scalar, read_vector, targets,
    out_scalars, out_vectors, out_scores, out_forces,
    codes, tables, turned, sources, picked, live, panel_s, panel_v, panel_p, gate_pos, rows_f, fwb, rv_col, rs_col, xsend, xrecv, own, ssend, recv,
    norm_buf, gather, energies, force_acc, force_recv, force_norm,
    codes_sem, panel_send, panel_recv, x_send, x_recv, s_send, s_recv,
    g_send, g_recv, f_send, e_send, e_recv, q_send, q_recv,
):
    row = lax.axis_index("rows")
    rep = lax.axis_index("reps")
    col = lax.axis_index("cols")
    total = rows * reps * cols
    me = (row * reps + rep) * cols + col
    s_ch = scalars.shape[0]
    v3 = vectors.shape[0]
    v_ch = v3 // 3
    blk = scalars.shape[1]
    slots = codes.shape[0]
    places = rows * cols
    windows = -(-slots // places)
    pose_pad = -(-poses // 8) * 8

    def peer(q):
        flat = lax.rem(me + q, total)
        return flat, {
            "rows": flat // (reps * cols),
            "reps": lax.rem(flat // cols, reps),
            "cols": lax.rem(flat, cols),
        }

    barrier = pltpu.get_barrier_semaphore()

    def greet(q, carry):
        pl.semaphore_signal(barrier, inc=1, device_id=peer(q)[1], device_id_type=MESH)
        return carry

    lax.fori_loop(1, total, greet, 0)
    codes_copy = pltpu.make_async_copy(codes_hbm, codes, codes_sem)
    codes_copy.start()

    panel_p[rep] = jnp.zeros((8, blk), F32)
    panel_p[rep, 0:3, :] = positions[...].astype(F32)
    panel_s[rep] = scalars[...]
    panel_v[rep] = vectors[...]
    lane_shell = lax.broadcasted_iota(jnp.int32, (shells, shells * blk), 1) // blk
    sub_shell = lax.broadcasted_iota(jnp.int32, (shells, shells * blk), 0)
    spread = jnp.where(lane_shell == sub_shell, 1.0, 0.0).astype(BF)
    fwb[...] = lax.dot_general(
        filter_weights[...], spread, (((0,), (0,)), ((), ())), preferred_element_type=F32
    )
    rv_row = jnp.concatenate([read_vector[...], jnp.zeros((1, 128 - v_ch), F32)], axis=1)
    rv_col[...] = jnp.transpose(jnp.broadcast_to(rv_row, (blk, 128)))[:v_ch]

    rs_col[...] = jnp.transpose(jnp.broadcast_to(read_scalar[...], (blk, s_ch)))

    pl.semaphore_wait(barrier, total - 1)

    def panel_copies(q, src_rep, which=(0, 1, 2)):
        out = []
        for a in which:
            buf = (panel_s, panel_v, panel_p)[a]
            out.append(
                pltpu.make_async_remote_copy(
                    src_ref=buf.at[src_rep],
                    dst_ref=buf.at[src_rep],
                    send_sem=panel_send.at[a, q],
                    recv_sem=panel_recv.at[a, src_rep],
                    device_id={"reps": q},
                    device_id_type=MESH,
                )
            )
        return out

    for o in range(1, reps):
        for c in panel_copies(lax.rem(rep + o, reps), rep):
            c.start()

    def make_rows(q, remote):
        if remote:
            panel_copies(q, q, (0,))[0].wait_recv()

        hidden = jnp.dot(weight_in[...], panel_s[q], preferred_element_type=F32)
        hidden = (hidden / (1.0 + jnp.exp(-hidden))).astype(BF)
        gates = jnp.dot(message_weight[...], hidden, preferred_element_type=F32).astype(BF)
        gates = gates.astype(F32)
        gs = gates[:s_ch]
        gv = gates[s_ch : s_ch + v_ch]
        gp = gates[s_ch + v_ch :]
        gate_pos[q] = gp
        if remote:
            for c in panel_copies(q, q, (1, 2)):
                c.wait_recv()

        pos = panel_p[q]
        vec = panel_v[q].astype(F32)
        gvv = [gv * vec[d * v_ch : (d + 1) * v_ch] for d in range(3)]
        gpp = [gp * pos[d : d + 1] for d in range(3)]
        for k in range(shells):
            span = pl.ds(k * blk, blk)
            rows_f[q, 1, :, span] = (gs * fwb[0:s_ch, span]).astype(BF)
            wv = fwb[s_ch : s_ch + v_ch, span]
            wp = fwb[s_ch + v_ch :, span]
            for d in range(3):
                rows_f[q, 0, d * v_ch : (d + 1) * v_ch, span] = (
                    gvv[d] * wv + gpp[d] * wp
                ).astype(BF)
            rows_f[q, 0, v3:, span] = (gp * wp).astype(BF)

    def find(dr, o, t):
        wanted = (lax.rem(row + dr, rows) * reps + rep) * cols + lax.rem(col + o, cols)
        slot = jnp.int32(0)
        found = jnp.int32(0)
        for e in range(t * places, min((t + 1) * places, slots)):
            hit = (target_block[e] == wanted) & (e < block_count[0])
            slot = jnp.where(hit, e, slot)
            found = jnp.where(hit, 1, found)
        return slot, found

    def table_step(dr, carry):
        for o in range(cols):
            for t in range(windows):
                slot, found = find(dr, o, t)
                sources[dr, o * windows + t] = lax.rem(source_block[slot] // cols, reps)
                picked[dr, o * windows + t] = slot
                live[dr, o * windows + t] = found
                code = codes[slot] * found
                for k in range(shells):
                    tables[dr, o * windows + t, k] = jnp.where(code == k + 1, 1.0, 0.0).astype(BF)
        return carry

    def turn_step(dr, carry):
        for o in range(cols):
            for t in range(windows):
                code = codes[picked[dr, o * windows + t]] * live[dr, o * windows + t]
                code = jnp.transpose(code.astype(F32))
                for k in range(shells):
                    turned[dr, o, k, :, t * blk : (t + 1) * blk] = jnp.where(
                        code == float(k + 1), 1.0, 0.0
                    ).astype(BF)
        return carry

    make_rows(rep, None)
    codes_copy.wait()
    lax.fori_loop(0, rows, table_step, 0)

    def rows_step(o, carry):
        make_rows(lax.rem(rep + o, reps), True)
        return carry

    lax.fori_loop(1, reps, rows_step, 0)

    def partial(h, dr, o):
        acc = None
        for t in range(windows):
            src = sources[dr, o * windows + t]
            table = tables[dr, o * windows + t].reshape(shells * blk, blk)
            term = jnp.dot(rows_f[src, h], table, preferred_element_type=F32)
            acc = term if acc is None else acc + term
        return acc

    def offset_of(u):
        s = lax.rem(u, rows)
        return jnp.where(s == rows - 1, 0, 1 + lax.rem(rows // 2 - 1 + s, rows - 1))

    def row_of(u):
        return lax.rem(row + offset_of(u), rows)

    def cross(s, o, arriving):
        if arriving:
            mine = o - 1
        else:
            mine = cols - o - 1
        return pltpu.make_async_remote_copy(
            src_ref=xsend.at[s, o - 1],
            dst_ref=xrecv.at[s, mine],
            send_sem=x_send.at[s, o - 1],
            recv_sem=x_recv.at[s, mine],
            device_id={"cols": lax.rem(col + o, cols)},
            device_id_type=MESH,
        )

    def along(u, src_row):
        h = u // rows
        return pltpu.make_async_remote_copy(
            src_ref=ssend.at[u],
            dst_ref=recv.at[h, src_row],
            send_sem=s_send.at[u],
            recv_sem=s_recv.at[h, src_row],
            device_id={"rows": row_of(u)},
            device_id_type=MESH,
        )

    def finish(u):
        for o in range(1, cols):
            cross(u, o, True).wait_recv()
        both = own[u]
        for o in range(1, cols):
            both = both + xrecv[u, o - 1].astype(F32)
        return both

    ahead = min(2, 2 * rows)

    def cross_step(u, carry):
        for o in range(1, cols):
            xsend[u, o - 1] = partial(u // rows, offset_of(u), o).astype(BF)
            cross(u, o, False).start()
        return carry

    def forward_step(u, carry):
        @pl.when(u + ahead < 2 * rows)
        def _():
            cross_step(u + ahead, 0)

        own[u] = partial(u // rows, offset_of(u), 0)

        @pl.when(lax.rem(u, rows) < rows - 1)
        def _():
            ssend[u] = finish(u).astype(BF)
            along(u, row).start()

        return carry

    lax.fori_loop(0, ahead, cross_step, 0)
    lax.fori_loop(0, 2 * rows, forward_step, 0)
    lax.fori_loop(0, rows, turn_step, 0)

    def arrive(h):
        own[h * rows + rows - 1] = finish(h * rows + rows - 1)
        for u in range(h * rows, h * rows + rows - 1):
            along(u, row_of(u)).wait_recv()

    def message(h, lo, hi):
        acc = own[h * rows + rows - 1, lo:hi]
        for s in range(rows - 1):
            acc = acc + recv[h, row_of(s), lo:hi].astype(F32)
        return acc

    arrive(0)
    norm = message(0, v3, v3 + v_ch)
    norm_buf[...] = norm
    pos_own = panel_p[rep]
    square = jnp.zeros((v_ch, blk), F32)
    for d in range(3):
        lo = d * v_ch
        nv = (
            vectors[lo : lo + v_ch].astype(F32)
            + message(0, lo, lo + v_ch)
            - pos_own[d : d + 1] * norm
        ).astype(BF)
        out_vectors[lo : lo + v_ch] = nv
        gather[row, col, lo : lo + v_ch] = nv
        nv = nv.astype(F32)
        square = square + nv * nv
    pose_row = node_pose[...]
    gather[row, col, v3 : v3 + 16] = jnp.broadcast_to(pose_row.astype(F32), (16, blk)).astype(BF)

    def spread_row(o, src_row):
        return pltpu.make_async_remote_copy(
            src_ref=gather.at[src_row, col],
            dst_ref=gather.at[src_row, col],
            send_sem=g_send.at[o],
            recv_sem=g_recv.at[src_row, col],
            device_id={"rows": lax.rem(row + o, rows)},
            device_id_type=MESH,
        )

    def spread_col(s, o, src_row, src_col):
        return pltpu.make_async_remote_copy(
            src_ref=gather.at[src_row, src_col],
            dst_ref=gather.at[src_row, src_col],
            send_sem=f_send.at[s, o - 1],
            recv_sem=g_recv.at[src_row, src_col],
            device_id={"cols": lax.rem(col + o, cols)},
            device_id_type=MESH,
        )

    for i in range(rows - 1):
        spread_row(i + 1, row).start()
    for o in range(1, cols):
        spread_col(0, o, row, col).start()

    vector_energy = jnp.sum(rv_col[...] * square, axis=0, keepdims=True)
    arrive(1)
    ns = (scalars[...].astype(F32) + message(1, 0, s_ch)).astype(BF)
    out_scalars[...] = ns
    energy = vector_energy + jnp.sum(rs_col[...] * ns.astype(F32), axis=0, keepdims=True)
    pose_iota = lax.broadcasted_iota(jnp.int32, (pose_pad, blk), 0)
    lane_iota = lax.broadcasted_iota(jnp.int32, (pose_pad, blk), 1)
    by_pose = jnp.sum(
        jnp.where(
            jnp.broadcast_to(pose_row, (pose_pad, blk)) == pose_iota,
            jnp.broadcast_to(energy, (pose_pad, blk)),
            0.0,
        ),
        axis=1,
        keepdims=True,
    )
    energies[me] = jnp.sum(
        jnp.where(lane_iota == pose_iota, jnp.broadcast_to(by_pose, (pose_pad, blk)), 0.0),
        axis=0,
        keepdims=True,
    )

    def energy_copy(q, src):
        return pltpu.make_async_remote_copy(
            src_ref=energies.at[src],
            dst_ref=energies.at[src],
            send_sem=e_send.at[q],
            recv_sem=e_recv.at[src],
            device_id=peer(q)[1],
            device_id_type=MESH,
        )

    def energy_start(q, carry):
        energy_copy(q, me).start()
        return carry

    def energy_wait(q, carry):
        energy_copy(q, peer(q)[0]).wait_recv()
        return carry

    lax.fori_loop(1, total, energy_start, 0)
    force_acc[...] = jnp.zeros_like(force_acc)
    for s in range(1, rows):
        r = lax.rem(row + s, rows)
        spread_row(1, r).wait_recv()
        for o in range(1, cols):
            spread_col(s, o, r, col).start()
    for s in range(rows):
        for o in range(1, cols):
            spread_col(s, o, lax.rem(row + s, rows), lax.rem(col + o, cols)).wait_recv()
    lax.fori_loop(1, total, energy_wait, 0)
    sums = energies[0]
    for q in range(1, total):
        sums = sums + energies[q]
    score_row = sums / POSE_ATOMS
    out_scores[...] = score_row[:, :poses]
    scores = jnp.broadcast_to(
        jnp.sum(
            jnp.where(
                lane_iota == pose_iota, jnp.broadcast_to(score_row, (pose_pad, blk)), 0.0
            ),
            axis=1,
            keepdims=True,
        ),
        (pose_pad, blk),
    )
    wanted = jnp.zeros((pose_pad, blk), F32)
    for p in range(poses):
        wanted = jnp.where(pose_iota == p, targets[p], wanted)
    resid = scores - wanted

    def gradient(r, c):
        pose = gather[r, c, v3 : v3 + 16].astype(F32)[0:1]
        member = jnp.broadcast_to(pose, (pose_pad, blk)) == pose_iota.astype(F32)
        node_resid = jnp.sum(jnp.where(member, resid, 0.0), axis=0, keepdims=True)
        scale = 2.0 * node_resid * rv_col[...]
        return [
            (scale * gather[r, c, d * v_ch : (d + 1) * v_ch].astype(F32)).astype(BF).astype(F32)
            for d in range(3)
        ]

    own_grad = gradient(row, col)
    for d in range(3):
        force_norm[d : d + 1] = jnp.sum(norm_buf[...] * own_grad[d], axis=0, keepdims=True)

    def backward(s, o):
        r, c = lax.rem(row + s, rows), lax.rem(col + o, cols)
        grad = gradient(r, c)
        weights = [fwb[s_ch + v_ch :, k * blk : (k + 1) * blk] for k in range(shells)]
        left = jnp.concatenate(
            [
                jnp.concatenate([(grad[d] * w).astype(BF) for w in weights], axis=1)
                for d in range(3)
            ],
            axis=0,
        )
        table = turned[s, o].reshape(shells * blk, windows * blk)
        back = jnp.dot(left, table, preferred_element_type=F32)
        for t in range(windows):
            src = sources[s, o * windows + t]
            gp = gate_pos[src]
            for d in range(3):
                piece = back[d * v_ch : (d + 1) * v_ch, t * blk : (t + 1) * blk]
                term = jnp.sum(gp * piece, axis=0, keepdims=True)
                for q in range(reps):
                    force_acc[q, d : d + 1] += jnp.where(src == q, term, 0.0)

    def backward_step(s, carry):
        for o in range(cols):
            backward(s, o)
        return carry

    lax.fori_loop(0, rows, backward_step, 0, unroll=4 if rows % 4 == 0 else 1)

    def force_copy(o, src):
        return pltpu.make_async_remote_copy(
            src_ref=force_acc.at[lax.rem(rep + o, reps)],
            dst_ref=force_recv.at[src],
            send_sem=q_send.at[o],
            recv_sem=q_recv.at[src],
            device_id={"reps": lax.rem(rep + o, reps)},
            device_id_type=MESH,
        )

    for o in range(1, reps):
        force_copy(o, rep).start()

    for o in range(1, reps):
        for c in panel_copies(lax.rem(rep + o, reps), rep):
            c.wait_send()
    for s in range(rows):
        for o in range(1, cols):
            spread_col(s, o, lax.rem(row + s, rows), col).wait_send()
        if s < rows - 1:
            spread_row(s + 1, row).wait_send()

    for u in range(2 * rows):
        for o in range(1, cols):
            cross(u, o, False).wait_send()
        if u % rows < rows - 1:
            along(u, row).wait_send()

    def energy_sent(q, carry):
        energy_copy(q, me).wait_send()
        return carry

    lax.fori_loop(1, total, energy_sent, 0)

    back = force_acc[rep]
    for o in range(1, reps):
        src = lax.rem(rep + o, reps)
        force_copy(o, src).wait_recv()
        back = back + force_recv[src]
    out_forces[...] = force_norm[0:3] - back[0:3]
    for o in range(1, reps):
        force_copy(o, rep).wait_send()


def publish(*refs):
    count = len(refs) // 2
    for source, target in zip(refs[:count], refs[count:]):
        target[...] = source[...]


def local(
    scalars, vectors, positions, node_pose, source_block, target_block, block_count, shell_codes,
    weight_in, message_weight, filter_weights, read_scalar, read_vector, targets,
):
    rows, reps, cols = (lax.axis_size(name) for name in ("rows", "reps", "cols"))
    total = rows * reps * cols
    s_ch, blk = scalars.shape
    v_ch = vectors.shape[1]
    v3 = 3 * v_ch
    half = s_ch
    shells = filter_weights.shape[0]
    slots = shell_codes.shape[0]
    poses = targets.shape[0]
    windows = -(-slots // (rows * cols))
    width = shells * blk
    vmem = pl.BlockSpec(memory_space=pltpu.VMEM)
    smem = pl.BlockSpec(memory_space=pltpu.SMEM)
    anywhere = pl.BlockSpec(memory_space=pl.ANY)
    dma = pltpu.SemaphoreType.DMA
    results = pl.pallas_call(
        functools.partial(kernel, rows, reps, cols, poses, shells),
        out_shape=(
            jax.ShapeDtypeStruct((s_ch, blk), BF),
            jax.ShapeDtypeStruct((v3, blk), BF),
            jax.ShapeDtypeStruct((1, poses), F32),
            jax.ShapeDtypeStruct((3, blk), F32),
        ),
        in_specs=[vmem] * 4 + [smem] * 3 + [anywhere] + [vmem] * 5 + [smem],
        out_specs=(vmem,) * 4,
        scratch_shapes=[
            pltpu.VMEM((slots, blk, blk), jnp.int32),
            pltpu.VMEM((rows, cols * windows, shells, blk, blk), BF),
            pltpu.VMEM((rows, cols, shells, blk, windows * blk), BF),
            pltpu.SMEM((rows, cols * windows), jnp.int32),
            pltpu.SMEM((rows, cols * windows), jnp.int32),
            pltpu.SMEM((rows, cols * windows), jnp.int32),
            pltpu.VMEM((reps, s_ch, blk), BF),
            pltpu.VMEM((reps, v3, blk), BF),
            pltpu.VMEM((reps, 8, blk), F32),
            pltpu.VMEM((reps, v_ch, blk), F32),
            pltpu.VMEM((reps, 2, half, width), BF),
            pltpu.VMEM((s_ch + 2 * v_ch, width), F32),
            pltpu.VMEM((v_ch, blk), F32),
            pltpu.VMEM((s_ch, blk), F32),
            pltpu.VMEM((2 * rows, cols - 1, half, blk), BF),
            pltpu.VMEM((2 * rows, cols - 1, half, blk), BF),
            pltpu.VMEM((2 * rows, half, blk), F32),
            pltpu.VMEM((2 * rows, half, blk), BF),
            pltpu.VMEM((2, rows, half, blk), BF),
            pltpu.VMEM((v_ch, blk), F32),
            pltpu.VMEM((rows, cols, v3 + 16, blk), BF),
            pltpu.VMEM((total, 1, blk), F32),
            pltpu.VMEM((reps, 8, blk), F32),
            pltpu.VMEM((reps, 8, blk), F32),
            pltpu.VMEM((8, blk), F32),
            dma,
            dma((3, reps)),
            dma((3, reps)),
            dma((2 * rows, cols - 1)),
            dma((2 * rows, cols - 1)),
            dma((2 * rows,)),
            dma((2, rows)),
            dma((rows,)),
            dma((rows, cols)),
            dma((rows, cols - 1)),
            dma((total,)),
            dma((total,)),
            dma((reps,)),
            dma((reps,)),
        ],
        compiler_params=pltpu.CompilerParams(
            collective_id=0, has_side_effects=True, vmem_limit_bytes=56 * 1024 * 1024
        ),
        name="layer",
    )(
        scalars, vectors.reshape(v3, blk), positions, node_pose.reshape(1, blk),
        source_block, target_block, block_count, shell_codes,
        weight_in, message_weight, filter_weights,
        read_scalar.reshape(1, s_ch), read_vector.reshape(1, v_ch), targets,
    )
    new_scalars, new_vectors, scores, forces = pl.pallas_call(
        publish,
        out_shape=tuple(jax.ShapeDtypeStruct(x.shape, x.dtype) for x in results),
        in_specs=[vmem] * 4,
        out_specs=(vmem,) * 4,
        name="publish",
    )(*results)
    return (
        new_scalars, new_vectors.reshape(3, v_ch, blk), scores.reshape(poses), forces,
    )


def solution(mesh):
    spread = ("groups", "rows", "reps", "cols")
    placed = (
        P(None, spread),
        P(None, None, spread),
        P(None, spread),
        P(spread),
        P(spread),
        P(spread),
        P(spread),
        P(spread, None, None),
        P(),
        P(),
        P(),
        P(),
        P(),
        P("groups"),
    )
    return jax.shard_map(
        local,
        mesh=mesh,
        in_specs=placed,
        out_specs=(P(None, spread), P(None, None, spread), P("groups"), P(None, spread)),
        check_vma=False,
    )
```
